128 devices in a mesh: row: 8 (over x, core), col: 16 (over z, y).
Axes of the slice: x: 4, y: 4, z: 4, core: 2. Of those that a mesh axis runs over, the one named last changes fastest.
Arguments:
- pair_in: bfloat16 [512, 512, 128], P('row', 'col'), may hold values from -6 to 6
- proj_weight: bfloat16 [2, 128, 512], replicated, may hold values from -0.5 to 0.5
- gate_weight: bfloat16 [2, 128, 128], replicated, may hold values from -0.5 to 0.5
- out_weight: bfloat16 [2, 128, 128], replicated, may hold values from -0.5 to 0.5
- block_mask: int32 [4, 4], replicated, may hold values 0 or 1
Outputs:
- pair_out: bfloat16 [512, 512, 128], P('row', 'col')
The draws below stay inside these ranges and needn't reach their ends.
Inputs may be any that keep to these rules, and one draw needn't show every extreme that they name: `block_mask`: 1 marks an active chain-pair block of 128 x 128 tokens, 0 an inactive one.
All inputs are finite; a program needn't handle non-finite values.
Results may differ from the reference program's by a relative error of at most 0.01.
Values may be sent and summed in bfloat16 or wider, within the bound.
A program may use at most 64 MiB of HBM per device.

```python
from functools import partial
import jax
import jax.numpy as jnp
from jax import lax

N = 512
C = 128
CH = 128
BLK = 128
NB = 4


def set_ends(array, own_key, low, high):
    dims = array.shape
    index_at = [jax.random.randint(jax.random.fold_in(own_key, axis), (), 0, dims[axis]) for axis in range(len(dims))]
    array = array.at[tuple(index_at)].set(low)
    longest = dims.index(max(dims))
    index_at[longest] = (index_at[longest] + 1) % dims[longest]
    return array.at[tuple(index_at)].set(high)


def shard_levels(own_key, extent, pieces, least, top_value):
    gain, own = 1.0, jax.random.fold_in(own_key, 6)
    for dim, parts in pieces:
        heights = jnp.exp(jax.random.uniform(jax.random.fold_in(own, dim), (parts,), jnp.float32, least / len(pieces), top_value / len(pieces)))
        gain = gain * jnp.repeat(heights, extent[dim] // parts).reshape([-1 if axis == dim else 1 for axis in range(len(extent))])
    return gain


def normal_values(own_key, shape, deviation, bound, shards=(), kind=jnp.bfloat16):
    entries = deviation * jax.random.normal(own_key, shape, jnp.float32)
    if shards:
        entries = entries * shard_levels(own_key, shape, shards, -0.22, 0.18)
    return jnp.clip(entries, -bound, bound).astype(kind)


def setup_inputs(seed: int = 0) -> dict:
    key_list = jax.random.split(jax.random.key(seed), 6)
    pair_in = normal_values(key_list[0], (N, N, C), 1.0, 6.0, ((0, 8), (1, 16)))
    proj_weight = normal_values(key_list[1], (2, C, 4 * CH), C ** -0.5, 0.5)
    gate_weight = normal_values(key_list[2], (2, C, C), C ** -0.5, 0.5)
    out_weight = normal_values(key_list[3], (2, CH, C), CH ** -0.5, 0.5)
    block_mask = set_ends((jax.random.randint(key_list[4], (NB, NB), 0, 4) < 3).astype(jnp.int32), jax.random.fold_in(key_list[4], 1), 0, 1)
    return dict(pair_in=pair_in, proj_weight=proj_weight, gate_weight=gate_weight, out_weight=out_weight, block_mask=block_mask)


epsilon = 1e-05

def layer_norm(values):
    center = values - lax.optimization_barrier(jnp.mean(values, axis=-1, keepdims=True))
    variance = lax.optimization_barrier(jnp.mean(center * center, axis=-1, keepdims=True))
    return center * lax.rsqrt(variance + epsilon)

def token_mask(block_mask):
    onehot = (jnp.arange(N, dtype=jnp.int32)[:, None] // BLK == jnp.arange(NB, dtype=jnp.int32)[None, :]).astype(jnp.float32)
    return jnp.dot(jnp.dot(onehot, block_mask.astype(jnp.float32)), onehot.T)

def project_block(w_proj, w_gate, inputs):
    block, mask_rows = inputs
    normed = layer_norm(block.astype(jnp.float32)).astype(jnp.bfloat16)
    flat = normed.reshape(-1, C)
    projected = jnp.dot(flat, w_proj, preferred_element_type=jnp.float32).reshape(BLK, N, 4 * CH)
    weight_mask = mask_rows[:, :, None]
    left_proj = (weight_mask * jax.nn.sigmoid(projected[..., CH:2 * CH]) * projected[..., :CH]).astype(jnp.bfloat16)
    right_proj = (weight_mask * jax.nn.sigmoid(projected[..., 3 * CH:]) * projected[..., 2 * CH:3 * CH]).astype(jnp.bfloat16)
    gate_value = jax.nn.sigmoid(jnp.dot(flat, w_gate, preferred_element_type=jnp.float32)).reshape(BLK, N, C)
    return (left_proj, right_proj, gate_value)

def outgoing_channel(operands):
    return jnp.dot(operands[0], operands[1].T, preferred_element_type=jnp.float32).astype(jnp.bfloat16)

def incoming_channel(operands):
    return jnp.dot(operands[0].T, operands[1], preferred_element_type=jnp.float32).astype(jnp.bfloat16)

def finish_block(w_out, inputs):
    block, triangle, gate_value, mask_rows = inputs
    tri_normed = layer_norm(triangle.astype(jnp.float32)).astype(jnp.bfloat16)
    update = jnp.dot(tri_normed.reshape(-1, CH), w_out, preferred_element_type=jnp.float32).reshape(BLK, N, C)
    return (block.astype(jnp.float32) + mask_rows[:, :, None] * gate_value * update).astype(jnp.bfloat16)

def reference(pair_in, proj_weight, gate_weight, out_weight, block_mask):
    pair_mask = token_mask(block_mask)
    mask_blocks = pair_mask.reshape(NB, BLK, N)
    pair = pair_in
    for direction in range(2):
        left_proj, right_proj, gate_value = lax.map(partial(project_block, proj_weight[direction], gate_weight[direction]), (pair.reshape(NB, BLK, N, C), mask_blocks))
        left_major = jnp.moveaxis(left_proj.reshape(N, N, CH), 2, 0)
        right_major = jnp.moveaxis(right_proj.reshape(N, N, CH), 2, 0)
        if direction == 0:
            triangle = lax.map(outgoing_channel, (left_major, right_major))
        else:
            triangle = lax.map(incoming_channel, (left_major, right_major))
        triangle = jnp.moveaxis(triangle, 0, 2).reshape(NB, BLK, N, CH)
        pair = lax.map(partial(finish_block, out_weight[direction]), (pair.reshape(NB, BLK, N, C), triangle, gate_value, mask_blocks)).reshape(N, N, C)
    return pair
```

```python
import jax
import jax.numpy as jnp
from jax import lax
from jax.experimental import pallas as pl
from jax.experimental.pallas import tpu as pltpu
from jax.sharding import PartitionSpec as P

MESH = pl.DeviceIdType.MESH
F32 = jnp.float32
BF16 = jnp.bfloat16
EPS = 1e-5

ROWS, COLS = 8, 16
DEVICES = ROWS * COLS
N = 512
C = 128
RI, CJ = 64, 32
JH = 16
TOK = RI * CJ
GROUPS = 4
GCH = DEVICES // GROUPS


def sigmoid(v):
    return 0.5 * jnp.tanh(0.5 * v) + 0.5


def norm_rows(v):
    center = v - jnp.mean(v, axis=0, keepdims=True)
    var = jnp.mean(center * center, axis=0, keepdims=True)
    return center * lax.rsqrt(var + EPS)


def coords(dst):
    return {"row": dst // COLS, "col": dst % COLS}


def kernel(
    pair_ref, wp_ref, wg_ref, wo_ref, mask_ref, out_ref,
    xf, pt, nt, gate, wpt, wgt, wot, fbuf, gbuf, mat, tri,
    s_lr0, s_lr1, r_lr0, r_lr1, s_t0, s_t1, r_t0, r_t1,
    send_sem, recv_sem,
):
    row, col = lax.axis_index("row"), lax.axis_index("col")
    me = row * COLS + col
    barrier = pltpu.get_barrier_semaphore()

    def greet(s, carry):
        dst = (me + s) % DEVICES
        pl.semaphore_signal(barrier, inc=1, device_id=coords(dst), device_id_type=MESH)
        return carry

    lax.fori_loop(1, DEVICES, greet, 0)

    mask = mask_ref[row // 2, col // 4].astype(F32)
    sends = ((s_lr0, s_t0), (s_lr1, s_t1))
    recvs = ((r_lr0, r_t0), (r_lr1, r_t1))

    def prepare_weights(t):
        for kind in range(4):
            w = wp_ref[t, :, kind * C : (kind + 1) * C].astype(F32).T.astype(BF16)
            for g in range(GROUPS):
                wpt[g, kind * GCH : (kind + 1) * GCH, :] = w[g * GCH : (g + 1) * GCH]
        wgt[...] = wg_ref[t].astype(F32).T.astype(BF16)
        wot[...] = wo_ref[t].astype(F32).T.astype(BF16)

    def send(t, what, dst):
        src, land = sends[t][what], recvs[t][what]
        pltpu.make_async_remote_copy(
            src_ref=src.at[dst],
            dst_ref=land.at[me],
            send_sem=send_sem.at[t, what],
            recv_sem=recv_sem.at[t, what],
            device_id=coords(dst),
            device_id_type=MESH,
        ).start()

    def wait(t, what, sem):
        land = recvs[t][what].at[pl.ds(0, DEVICES - 1)]
        pltpu.make_async_copy(land, land, sem.at[t, what]).wait()

    def project_and_send(t):
        src, land = sends[t][0], recvs[t][0]

        def group(step, carry):
            g = (step + row // 2 + col // 4 + col) % GROUPS
            w = wpt[g]
            for q in range(TOK // 256):
                v = jnp.dot(w, nt[:, q * 256 : (q + 1) * 256], preferred_element_type=F32)
                for side in range(2):
                    value = v[2 * side * GCH : (2 * side + 1) * GCH]
                    gates = v[(2 * side + 1) * GCH : (2 * side + 2) * GCH]
                    proj = mask * sigmoid(gates) * value
                    for half in range(2):
                        at = side * GCH * JH + 2 * q + half
                        fbuf[pl.ds(at, GCH, stride=JH), :] = proj[:, half * 128 : (half + 1) * 128]
            for side in range(2):
                tiles = fbuf[side * GCH * JH : (side + 1) * GCH * JH, :].astype(BF16)
                src[pl.ds(g * GCH, GCH), side] = tiles.reshape(GCH, JH, 128)

            def one(d, c):
                dst = g * GCH + (d + me) % GCH

                @pl.when(dst != me)
                def _():
                    send(t, 0, dst)

                return c

            lax.fori_loop(0, GCH, one, 0)
            return carry

        lax.fori_loop(0, GROUPS, group, 0)
        land[me] = src[me]

    def gates_of(t):
        for q in range(TOK // 256):
            sl = slice(q * 256, (q + 1) * 256)
            gate[:, sl] = mask * sigmoid(jnp.dot(wgt[...], nt[:, sl], preferred_element_type=F32))

    def triangle_and_send(t):
        land = recvs[t][0]
        src, back = sends[t][1], recvs[t][1]

        def relayout(c, carry):
            for side in range(2):
                for x in range(4):
                    a = land[(2 * x) * COLS + c, side]
                    b = land[(2 * x + 1) * COLS + c, side]
                    low = jnp.concatenate([a[:, :64], b[:, :64]], axis=1)
                    high = jnp.concatenate([a[:, 64:], b[:, 64:]], axis=1)
                    mat[side, pl.ds(c * CJ, JH), x * 128 : (x + 1) * 128] = low
                    mat[side, pl.ds(c * CJ + JH, JH), x * 128 : (x + 1) * 128] = high
            return carry

        lax.fori_loop(0, COLS, relayout, 0)
        for zj in range(4):
            js = slice(zj * 128, (zj + 1) * 128)
            if t == 0:
                v = lax.dot_general(mat[1, :, js], mat[0], (((0,), (0,)), ((), ())), preferred_element_type=F32)
            else:
                v = lax.dot_general(mat[1, js, :], mat[0], (((1,), (1,)), ((), ())), preferred_element_type=F32)
            tri[js, :] = v.astype(BF16)

        def chunk(step, carry):
            z = (step + row // 2 + col // 4 + col) % 4
            for y in range(4):
                c = z * 4 + y
                for x in range(4):
                    a = tri[pl.ds(c * CJ, JH), x * 128 : (x + 1) * 128]
                    b = tri[pl.ds(c * CJ + JH, JH), x * 128 : (x + 1) * 128]
                    src[(2 * x) * COLS + c] = jnp.concatenate([a[:, :64], b[:, :64]], axis=1)
                    src[(2 * x + 1) * COLS + c] = jnp.concatenate([a[:, 64:], b[:, 64:]], axis=1)

            def one(d, cc):
                e = (d + me) % 32
                dst = (e // 4) * COLS + z * 4 + e % 4

                @pl.when(dst != me)
                def _():
                    send(t, 1, dst)

                return cc

            lax.fori_loop(0, 32, one, 0)
            return carry

        lax.fori_loop(0, 4, chunk, 0)
        back[me] = src[me]

    def finish(t):
        back = recvs[t][1]

        def total(h, acc):
            return acc + back[h].astype(F32)

        mean = lax.fori_loop(0, DEVICES, total, jnp.zeros((JH, 128), F32), unroll=8) * (1.0 / DEVICES)

        def square(h, acc):
            d = back[h].astype(F32) - mean
            return acc + d * d

        var = lax.fori_loop(0, DEVICES, square, jnp.zeros((JH, 128), F32), unroll=8) * (1.0 / DEVICES)
        rstd = lax.rsqrt(var + EPS)

        def scale(h, carry):
            gbuf[pl.ds(pl.multiple_of(h * JH, JH), JH), :] = (back[h].astype(F32) - mean) * rstd
            return carry

        lax.fori_loop(0, DEVICES, scale, 0, unroll=8)
        for j in range(JH):
            sl = slice(j * 128, (j + 1) * 128)
            tn = gbuf[pl.ds(j, DEVICES, stride=JH), :].astype(BF16)
            update = jnp.dot(wot[...], tn, preferred_element_type=F32)
            new = (pt[:, sl] + gate[:, sl] * update).astype(BF16).astype(F32)
            if t == 0:
                pt[:, sl] = new
                nt[:, sl] = norm_rows(new).astype(BF16)
            else:
                back_t = new.T
                xf[pl.ds(j, RI, stride=CJ), :] = back_t[:RI]
                xf[pl.ds(j + JH, RI, stride=CJ), :] = back_t[RI:]

    xf[...] = pair_ref[...].reshape(TOK, C).astype(F32)
    for j in range(JH):
        sl = slice(j * 128, (j + 1) * 128)
        tokens = jnp.concatenate(
            [xf[pl.ds(j, RI, stride=CJ), :], xf[pl.ds(j + JH, RI, stride=CJ), :]], axis=0
        )
        v = tokens.T
        pt[:, sl] = v
        nt[:, sl] = norm_rows(v).astype(BF16)
    prepare_weights(0)
    pl.semaphore_wait(barrier, DEVICES - 1)
    for t in range(2):
        project_and_send(t)
        gates_of(t)
        wait(t, 0, recv_sem)
        triangle_and_send(t)
        wait(t, 1, recv_sem)
        finish(t)
        if t == 0:
            prepare_weights(1)
    for t in range(2):
        for what in range(2):
            wait(t, what, send_sem)
    out_ref[...] = xf[...].astype(BF16).reshape(RI, CJ, C)


def on_device(pair_in, proj_weight, gate_weight, out_weight, block_mask):
    lr = pltpu.VMEM((DEVICES, 2, JH, 128), BF16)
    tr = pltpu.VMEM((DEVICES, JH, 128), BF16)
    vmem = pl.BlockSpec(memory_space=pltpu.VMEM)
    return pl.pallas_call(
        kernel,
        out_shape=jax.ShapeDtypeStruct((RI, CJ, C), BF16),
        in_specs=[vmem, vmem, vmem, vmem, pl.BlockSpec(memory_space=pltpu.SMEM)],
        out_specs=vmem,
        scratch_shapes=[
            pltpu.VMEM((TOK, C), F32),
            pltpu.VMEM((C, TOK), F32),
            pltpu.VMEM((C, TOK), BF16),
            pltpu.VMEM((C, TOK), F32),
            pltpu.VMEM((GROUPS, 4 * GCH, C), BF16),
            pltpu.VMEM((C, C), BF16),
            pltpu.VMEM((C, C), BF16),
            pltpu.VMEM((2 * GCH * JH, 128), F32),
            pltpu.VMEM((DEVICES * JH, 128), F32),
            pltpu.VMEM((2, N, N), BF16),
            pltpu.VMEM((N, N), BF16),
            lr, lr, lr, lr, tr, tr, tr, tr,
            pltpu.SemaphoreType.DMA((2, 2)),
            pltpu.SemaphoreType.DMA((2, 2)),
        ],
        compiler_params=pltpu.CompilerParams(
            collective_id=0, has_side_effects=True, vmem_limit_bytes=40 * 2**20
        ),
        name="triangle_pair",
    )(pair_in, proj_weight, gate_weight, out_weight, block_mask)


def solution(mesh):
    placed = (P("row", "col", None), P(), P(), P(), P())
    return jax.shard_map(
        on_device, mesh=mesh, in_specs=placed, out_specs=P("row", "col", None), check_vma=False
    )
```

```python
import jax
import jax.numpy as jnp
from jax import lax
from jax.experimental import pallas as pl
from jax.experimental.pallas import tpu as pltpu
from jax.sharding import PartitionSpec as P

MESH = pl.DeviceIdType.MESH
F32 = jnp.float32
BF16 = jnp.bfloat16
EPS = 1e-5

ROWS, COLS = 8, 16
DEVICES = ROWS * COLS
N = 512
C = 128
RI, CJ = 64, 32
JH = 16
TOK = RI * CJ
PLANE = COLS
STEPS = 4
AROUND = [((a + b) % 4, a) for b in range(4) for a in range(4)]


def sigmoid(v):
    return 0.5 * jnp.tanh(0.5 * v) + 0.5


def norm_rows(v):
    center = v - jnp.mean(v, axis=0, keepdims=True)
    var = jnp.mean(center * center, axis=0, keepdims=True)
    return center * lax.rsqrt(var + EPS)


def wrap4(v):
    return jnp.where(v >= 4, v - 4, v)


def kernel(
    pair_hbm, wp_hbm, wg_hbm, wo_hbm, mask_ref, out_ref,
    pair_ref, wp_ref, wg_ref, wo_ref,
    xf, pt, nt, gate, wpt, wgt, wot, fbuf, gbuf, mat, tri,
    s_lr0, s_lr1, r_lr0, r_lr1, s_t0, s_t1, r_t0, r_t1,
    send_sem, recv_sem, load_sem,
):
    row, col = lax.axis_index("row"), lax.axis_index("col")
    loads = [
        pltpu.make_async_copy(src, dst, load_sem.at[i])
        for i, (src, dst) in enumerate(
            [(pair_hbm, pair_ref), (wp_hbm, wp_ref), (wg_hbm, wg_ref), (wo_hbm, wo_ref)]
        )
    ]
    for load in loads:
        load.start()
    x, core = row // 2, row % 2
    z, y = col // 4, col % 4
    me = core * 64 + x * COLS + col
    zs = [z if d == 0 else wrap4(z + d) for d in range(4)]
    ys = [y if d == 0 else wrap4(y + d) for d in range(4)]
    cols = {(dz, dy): zs[dz] * 4 + ys[dy] for dz in range(4) for dy in range(4)}
    flip = (z + y) % 2
    barrier = pltpu.get_barrier_semaphore()

    def greet(s, carry):
        r2 = jnp.where(row + s >= ROWS, row + s - ROWS, row + s)
        for dz, dy in AROUND:
            there = {"row": r2, "col": cols[dz, dy]}
            if (dz, dy) == (0, 0):

                @pl.when(s != 0)
                def _():
                    pl.semaphore_signal(barrier, inc=1, device_id=there, device_id_type=MESH)
            else:
                pl.semaphore_signal(barrier, inc=1, device_id=there, device_id_type=MESH)
        return carry

    lax.fori_loop(0, ROWS, greet, 0)

    mask = mask_ref[x, z].astype(F32)
    sends = ((s_lr0, s_t0), (s_lr1, s_t1))
    recvs = ((r_lr0, r_t0), (r_lr1, r_t1))

    def prepare_weights(t):
        for kind in range(4):
            w = wp_ref[t, :, kind * C : (kind + 1) * C].astype(F32).T.astype(BF16)
            for g in range(DEVICES // PLANE):
                wpt[g, kind * PLANE : (kind + 1) * PLANE, :] = w[g * PLANE : (g + 1) * PLANE]
        wgt[...] = wg_ref[t].astype(F32).T.astype(BF16)
        wot[...] = wo_ref[t].astype(F32).T.astype(BF16)

    def planes_of(pair):
        e = (pair + flip) % 2
        return [wrap4(x + e), wrap4(wrap4(x + e) + 2)]

    def send_group(t, what, k, planes):
        src, land = sends[t][what], recvs[t][what]
        for dz, dy in AROUND:
            for x2 in planes:
                c2 = cols[dz, dy]
                slot = k * 64 + x2 * COLS + c2
                copy = pltpu.make_async_remote_copy(
                    src_ref=src.at[slot],
                    dst_ref=land.at[me],
                    send_sem=send_sem.at[t, what],
                    recv_sem=recv_sem.at[t, what],
                    device_id={"row": 2 * x2 + k, "col": c2},
                    device_id_type=MESH,
                )
                if (dz, dy) == (0, 0):
                    pl.when(slot != me)(copy.start)
                else:
                    copy.start()

    def wait(t, what, sem):
        land = recvs[t][what].at[pl.ds(0, DEVICES - 1)]
        pltpu.make_async_copy(land, land, sem.at[t, what]).wait()

    def project_and_send(t):
        src, land = sends[t][0], recvs[t][0]
        size = PLANE * JH

        def group(step, carry):
            k = step // 2
            planes = planes_of(step % 2)
            w = jnp.concatenate([wpt[k * 4 + x2] for x2 in planes], axis=0)
            for q in range(TOK // 256):
                v = jnp.dot(w, nt[:, q * 256 : (q + 1) * 256], preferred_element_type=F32)
                for p in range(2):
                    for side in range(2):
                        at = p * 4 * PLANE + 2 * side * PLANE
                        proj = mask * sigmoid(v[at + PLANE : at + 2 * PLANE]) * v[at : at + PLANE]
                        for half in range(2):
                            to = (2 * p + side) * size + 2 * q + half
                            fbuf[pl.ds(to, PLANE, stride=JH), :] = proj[:, half * 128 : (half + 1) * 128]
            for p in range(2):
                for side in range(2):
                    at = (2 * p + side) * size
                    tiles = fbuf[at : at + size, :].astype(BF16).reshape(PLANE, JH, 128)
                    src[pl.ds(k * 64 + planes[p] * COLS, PLANE), side] = tiles
            send_group(t, 0, k, planes)
            return carry

        lax.fori_loop(0, STEPS, group, 0)
        land[me] = src[me]

    def gates_of(t):
        for q in range(TOK // 256):
            sl = slice(q * 256, (q + 1) * 256)
            gate[:, sl] = mask * sigmoid(jnp.dot(wgt[...], nt[:, sl], preferred_element_type=F32))

    def triangle_and_send(t):
        land = recvs[t][0]
        src, back = sends[t][1], recvs[t][1]

        def relayout(c, carry):
            for side in range(2):
                for x2 in range(4):
                    a = land[x2 * COLS + c, side]
                    b = land[64 + x2 * COLS + c, side]
                    low = jnp.concatenate([a[:, :64], b[:, :64]], axis=1)
                    high = jnp.concatenate([a[:, 64:], b[:, 64:]], axis=1)
                    mat[side, pl.ds(c * CJ, JH), x2 * 128 : (x2 + 1) * 128] = low
                    mat[side, pl.ds(c * CJ + JH, JH), x2 * 128 : (x2 + 1) * 128] = high
            return carry

        lax.fori_loop(0, COLS, relayout, 0, unroll=4)
        for zj in range(4):
            js = slice(zj * 128, (zj + 1) * 128)
            if t == 0:
                v = lax.dot_general(mat[1, :, js], mat[0], (((0,), (0,)), ((), ())), preferred_element_type=F32)
            else:
                v = lax.dot_general(mat[1, js, :], mat[0], (((1,), (1,)), ((), ())), preferred_element_type=F32)
            v = v.astype(BF16)
            for x2 in range(4):
                tri[x2, js, :] = v[:, x2 * 128 : (x2 + 1) * 128]
        for k in range(2):
            lanes = slice(k * 64, (k + 1) * 64)

            def chunk(pair, carry):
                planes = planes_of(pair)
                for x2 in planes:
                    for c in range(COLS):
                        a = tri[x2, c * CJ : c * CJ + JH, lanes]
                        b = tri[x2, c * CJ + JH : (c + 1) * CJ, lanes]
                        src[k * 64 + x2 * COLS + c] = jnp.concatenate([a, b], axis=1)
                send_group(t, 1, k, planes)
                return carry

            lax.fori_loop(0, 2, chunk, 0)
        back[me] = src[me]

    def finish(t):
        back = recvs[t][1]

        def total(h, acc):
            return acc + back[h].astype(F32)

        mean = lax.fori_loop(0, DEVICES, total, jnp.zeros((JH, 128), F32), unroll=8) * (1.0 / DEVICES)

        def square(h, acc):
            d = back[h].astype(F32) - mean
            return acc + d * d

        var = lax.fori_loop(0, DEVICES, square, jnp.zeros((JH, 128), F32), unroll=8) * (1.0 / DEVICES)
        rstd = lax.rsqrt(var + EPS)

        def scale(h, carry):
            gbuf[pl.ds(pl.multiple_of(h * JH, JH), JH), :] = (back[h].astype(F32) - mean) * rstd
            return carry

        lax.fori_loop(0, DEVICES, scale, 0, unroll=8)
        for j in range(JH):
            sl = slice(j * 128, (j + 1) * 128)
            tn = gbuf[pl.ds(j, DEVICES, stride=JH), :].astype(BF16)
            update = jnp.dot(wot[...], tn, preferred_element_type=F32)
            new = (pt[:, sl] + gate[:, sl] * update).astype(BF16).astype(F32)
            if t == 0:
                pt[:, sl] = new
                nt[:, sl] = norm_rows(new).astype(BF16)
            else:
                back_t = new.T
                xf[pl.ds(j, RI, stride=CJ), :] = back_t[:RI]
                xf[pl.ds(j + JH, RI, stride=CJ), :] = back_t[RI:]

    loads[0].wait()
    xf[...] = pair_ref[...].reshape(TOK, C).astype(F32)
    for j in range(JH):
        sl = slice(j * 128, (j + 1) * 128)
        tokens = jnp.concatenate(
            [xf[pl.ds(j, RI, stride=CJ), :], xf[pl.ds(j + JH, RI, stride=CJ), :]], axis=0
        )
        v = tokens.T
        pt[:, sl] = v
        nt[:, sl] = norm_rows(v).astype(BF16)
    for load in loads[1:]:
        load.wait()
    prepare_weights(0)
    pl.semaphore_wait(barrier, DEVICES - 1)
    for t in range(2):
        project_and_send(t)
        gates_of(t)
        wait(t, 0, recv_sem)
        triangle_and_send(t)
        wait(t, 1, recv_sem)
        finish(t)
        if t == 0:
            prepare_weights(1)
    for t in range(2):
        for what in range(2):
            wait(t, what, send_sem)
    out_ref[...] = xf[...].astype(BF16).reshape(RI, CJ, C)


def on_device(pair_in, proj_weight, gate_weight, out_weight, block_mask):
    lr = pltpu.VMEM((DEVICES, 2, JH, 128), BF16)
    tr = pltpu.VMEM((DEVICES, JH, 128), BF16)
    vmem = pl.BlockSpec(memory_space=pltpu.VMEM)
    hbm = pl.BlockSpec(memory_space=pl.ANY)
    return pl.pallas_call(
        kernel,
        out_shape=jax.ShapeDtypeStruct((RI, CJ, C), BF16),
        in_specs=[hbm, hbm, hbm, hbm, pl.BlockSpec(memory_space=pltpu.SMEM)],
        out_specs=vmem,
        scratch_shapes=[
            pltpu.VMEM(pair_in.shape, BF16),
            pltpu.VMEM(proj_weight.shape, BF16),
            pltpu.VMEM(gate_weight.shape, BF16),
            pltpu.VMEM(out_weight.shape, BF16),
            pltpu.VMEM((TOK, C), F32),
            pltpu.VMEM((C, TOK), F32),
            pltpu.VMEM((C, TOK), BF16),
            pltpu.VMEM((C, TOK), F32),
            pltpu.VMEM((DEVICES // PLANE, 4 * PLANE, C), BF16),
            pltpu.VMEM((C, C), BF16),
            pltpu.VMEM((C, C), BF16),
            pltpu.VMEM((4 * PLANE * JH, 128), F32),
            pltpu.VMEM((DEVICES * JH, 128), F32),
            pltpu.VMEM((2, N, N), BF16),
            pltpu.VMEM((4, N, 128), BF16),
            lr, lr, lr, lr, tr, tr, tr, tr,
            pltpu.SemaphoreType.DMA((2, 2)),
            pltpu.SemaphoreType.DMA((2, 2)),
            pltpu.SemaphoreType.DMA((4,)),
        ],
        compiler_params=pltpu.CompilerParams(
            collective_id=0, has_side_effects=True, vmem_limit_bytes=60 * 2**20
        ),
        name="triangle_pair",
    )(pair_in, proj_weight, gate_weight, out_weight, block_mask)


def solution(mesh):
    placed = (P("row", "col", None), P(), P(), P(), P())
    return jax.shard_map(
        on_device, mesh=mesh, in_specs=placed, out_specs=P("row", "col", None), check_vma=False
    )
```

```python
import jax
import jax.numpy as jnp
from jax import lax
from jax.experimental import pallas as pl
from jax.experimental.pallas import tpu as pltpu
from jax.sharding import PartitionSpec as P

MESH = pl.DeviceIdType.MESH
F32 = jnp.float32
BF16 = jnp.bfloat16
EPS = 1e-5

ROWS, COLS = 8, 16
DEVICES = ROWS * COLS
N = 512
C = 128
RI, CJ = 64, 32
JH = 16
TOK = RI * CJ
PLANE = COLS


def hops(offset):
    return sum(min(d, 4 - d) for d in offset)


HALVES = [
    sorted(
        ((p, (a + b) % 4, a) for b in range(4) for a in range(4) for p in range(2)),
        key=lambda o: -(hop[o[0]] + hops(o[1:])),
    )
    for hop in ((2, 1), (1, 0))
]
IN_PLANE = sorted((((a + b) % 4, a) for b in range(4) for a in range(4)), key=lambda o: -hops(o))
FAR_FIRST = sorted(
    ((a, (a + b) % 4, (a + c) % 4) for b in range(4) for c in range(4) for a in range(4)),
    key=lambda offset: -hops(offset),
)


def sigmoid(v):
    return 0.5 * jnp.tanh(0.5 * v) + 0.5


def norm_rows(v):
    center = v - jnp.mean(v, axis=0, keepdims=True)
    var = jnp.mean(center * center, axis=0, keepdims=True)
    return center * lax.rsqrt(var + EPS)


def wrap4(v):
    return jnp.where(v >= 4, v - 4, v)


def kernel(
    pair_hbm, wp_hbm, wg_hbm, wo_hbm, mask_ref, out_ref,
    pair_ref, wp_ref, wg_ref, wo_ref,
    xf, pt, nt, gate, wpt, wgt, wot, fbuf, gbuf, mat,
    s_lr0, s_lr1, r_lr0, r_lr1, s_t0, s_t1, r_t0, r_t1,
    send_sem, recv_sem, load_sem,
):
    row, col = lax.axis_index("row"), lax.axis_index("col")
    loads = [
        pltpu.make_async_copy(src, dst, load_sem.at[i])
        for i, (src, dst) in enumerate(
            [(pair_hbm, pair_ref), (wp_hbm, wp_ref), (wg_hbm, wg_ref), (wo_hbm, wo_ref)]
        )
    ]
    for load in loads:
        load.start()
    x, core = row // 2, row % 2
    z, y = col // 4, col % 4
    me = core * 64 + x * COLS + col
    xs, zs, ys = ([v if d == 0 else wrap4(v + d) for d in range(4)] for v in (x, z, y))
    cols = {(dz, dy): zs[dz] * 4 + ys[dy] for dz in range(4) for dy in range(4)}
    xa, xb = jnp.where((z + y) % 2 == 0, xs[1], xs[3]), jnp.where((z + y) % 2 == 0, xs[3], xs[1])
    za, zb = jnp.where((x + y) % 2 == 0, zs[1], zs[3]), jnp.where((x + y) % 2 == 0, zs[3], zs[1])
    barrier = pltpu.get_barrier_semaphore()

    for dx, dz, dy in FAR_FIRST:
        for k in range(2):
            row2 = 2 * xs[dx] + (k if dx or dz or dy else 1 - core)
            if (dx, dz, dy) != (0, 0, 0) or k == 0:
                there = {"row": row2, "col": cols[dz, dy]}
                pl.semaphore_signal(barrier, inc=1, device_id=there, device_id_type=MESH)

    mask = mask_ref[x, z].astype(F32)
    sends = ((s_lr0, s_t0), (s_lr1, s_t1))
    recvs = ((r_lr0, r_t0), (r_lr1, r_t1))

    def prepare_weights(t):
        for kind in range(4):
            w = wp_ref[t, :, kind * C : (kind + 1) * C].astype(F32).T.astype(BF16)
            for g in range(DEVICES // PLANE):
                wpt[g, kind * PLANE : (kind + 1) * PLANE, :] = w[g * PLANE : (g + 1) * PLANE]
        wgt[...] = wg_ref[t].astype(F32).T.astype(BF16)
        wot[t] = wo_ref[t].astype(F32).T.astype(BF16)

    def send(t, what, k, x2, c2, own):
        src, land = sends[t][what], recvs[t][what]
        slot = k * 64 + x2 * COLS + c2
        copy = pltpu.make_async_remote_copy(
            src_ref=src.at[slot],
            dst_ref=land.at[me],
            send_sem=send_sem.at[t, what, k],
            recv_sem=recv_sem.at[t, what],
            device_id={"row": 2 * x2 + k, "col": c2},
            device_id_type=MESH,
        )
        if own:
            keep = pltpu.make_async_copy(src.at[slot], land.at[me], send_sem.at[t, what, k])
            pl.when(core != k)(copy.start)
            pl.when(core == k)(keep.start)
        else:
            copy.start()

    def wait_sent(t, what, k):
        src = sends[t][what].at[pl.ds(0, 64)]
        pltpu.make_async_copy(src, src, send_sem.at[t, what, k]).wait()

    def wait_arrived(t, what):
        wait_sent(t, what, core)
        land = recvs[t][what].at[pl.ds(0, DEVICES - 1)]
        pltpu.make_async_copy(land, land, recv_sem.at[t, what]).wait()

    halves = ((xs[2], xa), (xb, xs[0]))

    def project(t, k, half):
        src = sends[t][0]
        size = PLANE * JH
        planes = halves[half]
        w = jnp.concatenate([wpt[k * 4 + x2] for x2 in planes], axis=0)
        for q in range(TOK // 256):
            v = jnp.dot(w, nt[:, q * 256 : (q + 1) * 256], preferred_element_type=F32)
            for p in range(2):
                for side in range(2):
                    at = p * 4 * PLANE + 2 * side * PLANE
                    proj = mask * sigmoid(v[at + PLANE : at + 2 * PLANE]) * v[at : at + PLANE]
                    for half in range(2):
                        to = (2 * p + side) * size + 2 * q + half
                        fbuf[pl.ds(to, PLANE, stride=JH), :] = proj[:, half * 128 : (half + 1) * 128]
        for p in range(2):
            for side in range(2):
                at = (2 * p + side) * size
                tiles = fbuf[at : at + size, :].astype(BF16).reshape(PLANE, JH, 128)
                src[pl.ds(k * 64 + planes[p] * COLS, PLANE), side] = tiles

    def send_half(t, k, half):
        for p, dz, dy in HALVES[half]:
            send(t, 0, k, halves[half][p], cols[dz, dy], (half, p, dz, dy) == (1, 1, 0, 0))

    def gates_of(t):
        for q in range(TOK // 256):
            sl = slice(q * 256, (q + 1) * 256)
            gate[:, sl] = mask * sigmoid(jnp.dot(wgt[...], nt[:, sl], preferred_element_type=F32))

    def triangle_and_send(t):
        land = recvs[t][0]
        src = sends[t][1]

        def relayout(c, carry):
            rows = pl.ds(pl.multiple_of(c * CJ, CJ), JH), pl.ds(pl.multiple_of(c * CJ + JH, JH), JH)
            for side in range(2):
                for x2 in range(4):
                    a = land[x2 * COLS + c, side]
                    b = land[64 + x2 * COLS + c, side]
                    mat[side, x2, rows[0]] = jnp.concatenate([a[:, :64], b[:, :64]], axis=1)
                    mat[side, x2, rows[1]] = jnp.concatenate([a[:, 64:], b[:, 64:]], axis=1)
            return carry

        lax.fori_loop(0, COLS, relayout, 0, unroll=4)
        left = jnp.concatenate([mat[0, x2] for x2 in range(4)], axis=1)
        for dz, z2 in ((2, zs[2]), (1, za), (3, zb), (0, zs[0])):
            if t == 0:
                v = lax.dot_general(mat[1, z2], left, (((0,), (0,)), ((), ())), preferred_element_type=F32)
            else:
                js = pl.ds(pl.multiple_of(z2 * 128, 128), 128)
                right = jnp.concatenate([mat[1, x2, js] for x2 in range(4)], axis=1)
                v = lax.dot_general(right, left, (((1,), (1,)), ((), ())), preferred_element_type=F32)
            v = v.astype(BF16)
            for k in range(2):
                for x2 in range(4):
                    lanes = slice(x2 * 128 + k * 64, x2 * 128 + (k + 1) * 64)
                    for y2 in range(4):
                        a = v[y2 * CJ : y2 * CJ + JH, lanes]
                        b = v[y2 * CJ + JH : (y2 + 1) * CJ, lanes]
                        src[k * 64 + x2 * COLS + z2 * 4 + y2] = jnp.concatenate([a, b], axis=1)
            for dx, dy in IN_PLANE:
                for k in range(2):
                    send(t, 1, k, xs[dx], z2 * 4 + ys[dy], (dx, dz, dy) == (0, 0, 0))

    def finish(t):
        back = recvs[t][1]

        zero = jnp.zeros((JH, 128), F32)

        def total(i, acc):
            return tuple(a + back[4 * i + n].astype(F32) for n, a in enumerate(acc))

        acc = lax.fori_loop(0, DEVICES // 4, total, (zero,) * 4, unroll=4)
        mean = ((acc[0] + acc[1]) + (acc[2] + acc[3])) * (1.0 / DEVICES)

        def square(i, acc):
            new = []
            for n, a in enumerate(acc):
                h = 4 * i + n
                d = back[h].astype(F32) - mean
                gbuf[pl.ds(pl.multiple_of(h * JH, JH), JH), :] = d
                new.append(a + d * d)
            return tuple(new)

        acc = lax.fori_loop(0, DEVICES // 4, square, (zero,) * 4, unroll=4)
        var = ((acc[0] + acc[1]) + (acc[2] + acc[3])) * (1.0 / DEVICES)
        rstd = lax.rsqrt(var + EPS)
        for j in range(JH):
            sl = slice(j * 128, (j + 1) * 128)
            tn = gbuf[pl.ds(j, DEVICES, stride=JH), :].astype(BF16)
            update = jnp.dot(wot[t], tn, preferred_element_type=F32)
            new = (pt[:, sl] + gate[:, sl] * (rstd[j : j + 1] * update)).astype(BF16).astype(F32)
            if t == 0:
                pt[:, sl] = new
                nt[:, sl] = norm_rows(new).astype(BF16)
            else:
                back_t = new.T
                xf[pl.ds(j, RI, stride=CJ), :] = back_t[:RI]
                xf[pl.ds(j + JH, RI, stride=CJ), :] = back_t[RI:]

    loads[0].wait()
    xf[...] = pair_ref[...].reshape(TOK, C).astype(F32)
    for j in range(JH):
        sl = slice(j * 128, (j + 1) * 128)
        tokens = jnp.concatenate(
            [xf[pl.ds(j, RI, stride=CJ), :], xf[pl.ds(j + JH, RI, stride=CJ), :]], axis=0
        )
        v = tokens.T
        pt[:, sl] = v
        nt[:, sl] = norm_rows(v).astype(BF16)
    for load in loads[1:]:
        load.wait()
    prepare_weights(0)
    project(0, 0, 0)
    pl.semaphore_wait(barrier, DEVICES - 1)
    for t in range(2):
        for k in range(2):
            for half in range(2):
                if (t, k, half) != (0, 0, 0):
                    project(t, k, half)
            for dx, dz, dy in FAR_FIRST:
                send(t, 0, k, xs[dx], cols[dz, dy], (dx, dz, dy) == (0, 0, 0))
        gates_of(t)
        if t == 0:
            prepare_weights(1)
        wait_arrived(t, 0)
        triangle_and_send(t)
        wait_arrived(t, 1)
        finish(t)
        for what in range(2):
            wait_sent(t, what, 1 - core)
    out_ref[...] = xf[...].astype(BF16).reshape(RI, CJ, C)


def on_device(pair_in, proj_weight, gate_weight, out_weight, block_mask):
    lr = pltpu.VMEM((DEVICES, 2, JH, 128), BF16)
    tr = pltpu.VMEM((DEVICES, JH, 128), BF16)
    vmem = pl.BlockSpec(memory_space=pltpu.VMEM)
    hbm = pl.BlockSpec(memory_space=pl.ANY)
    return pl.pallas_call(
        kernel,
        out_shape=jax.ShapeDtypeStruct((RI, CJ, C), BF16),
        in_specs=[hbm, hbm, hbm, hbm, pl.BlockSpec(memory_space=pltpu.SMEM)],
        out_specs=vmem,
        scratch_shapes=[
            pltpu.VMEM(pair_in.shape, BF16),
            pltpu.VMEM(proj_weight.shape, BF16),
            pltpu.VMEM(gate_weight.shape, BF16),
            pltpu.VMEM(out_weight.shape, BF16),
            pltpu.VMEM((TOK, C), F32),
            pltpu.VMEM((C, TOK), F32),
            pltpu.VMEM((C, TOK), BF16),
            pltpu.VMEM((C, TOK), F32),
            pltpu.VMEM((DEVICES // PLANE, 4 * PLANE, C), BF16),
            pltpu.VMEM((C, C), BF16),
            pltpu.VMEM((2, C, C), BF16),
            pltpu.VMEM((4 * PLANE * JH, 128), F32),
            pltpu.VMEM((DEVICES * JH, 128), F32),
            pltpu.VMEM((2, 4, N, 128), BF16),
            lr, lr, lr, lr, tr, tr, tr, tr,
            pltpu.SemaphoreType.DMA((2, 2, 2)),
            pltpu.SemaphoreType.DMA((2, 2)),
            pltpu.SemaphoreType.DMA((4,)),
        ],
        compiler_params=pltpu.CompilerParams(
            collective_id=0, has_side_effects=True, vmem_limit_bytes=60 * 2**20
        ),
        name="triangle_pair",
    )(pair_in, proj_weight, gate_weight, out_weight, block_mask)


def solution(mesh):
    placed = (P("row", "col", None), P(), P(), P(), P())
    return jax.shard_map(
        on_device, mesh=mesh, in_specs=placed, out_specs=P("row", "col", None), check_vma=False
    )
```

```python
import jax
import jax.numpy as jnp
from jax import lax
from jax.experimental import pallas as pl
from jax.experimental.pallas import tpu as pltpu
from jax.sharding import PartitionSpec as P

MESH = pl.DeviceIdType.MESH
F32 = jnp.float32
BF16 = jnp.bfloat16
EPS = 1e-5

ROWS, COLS = 8, 16
DEVICES = ROWS * COLS
N = 512
C = 128
RI, CJ = 64, 32
JH = 16
TOK = RI * CJ
PLANE = COLS


def hops(offset):
    return sum(min(d, 4 - d) for d in offset)


HALVES = [
    sorted(
        ((p, (a + b) % 4, a) for b in range(4) for a in range(4) for p in range(2)),
        key=lambda o: -(hop[o[0]] + hops(o[1:])),
    )
    for hop in ((2, 1), (1, 0))
]
IN_PLANE = sorted((((a + b) % 4, a) for b in range(4) for a in range(4)), key=lambda o: -hops(o))
FAR_FIRST = sorted(
    ((a, (a + b) % 4, (a + c) % 4) for b in range(4) for c in range(4) for a in range(4)),
    key=lambda offset: -hops(offset),
)


def sigmoid(v):
    return 0.5 * jnp.tanh(0.5 * v) + 0.5


def norm_rows(v):
    center = v - jnp.mean(v, axis=0, keepdims=True)
    var = jnp.mean(center * center, axis=0, keepdims=True)
    return center * lax.rsqrt(var + EPS)


def wrap4(v):
    return jnp.where(v >= 4, v - 4, v)


def kernel(
    pair_hbm, wp_hbm, wg_hbm, wo_hbm, mask_hbm, out_ref,
    pair_ref, wp_ref, wg_ref, wo_ref, mask_ref,
    xf, pt, nt, gate, wpt, wgt, wot, wsum, upd, fbuf, gbuf, mat,
    s_lr0, s_lr1, r_lr0, r_lr1, s_t0, s_t1, r_t0, r_t1,
    send_sem, recv_sem, load_sem,
):
    row, col = lax.axis_index("row"), lax.axis_index("col")
    loads = [
        pltpu.make_async_copy(src, dst, load_sem.at[i])
        for i, (src, dst) in enumerate(
            [(pair_hbm, pair_ref), (mask_hbm, mask_ref), (wp_hbm, wp_ref), (wg_hbm, wg_ref), (wo_hbm, wo_ref)]
        )
    ]
    for load in loads:
        load.start()
    x, core = row // 2, row % 2
    z, y = col // 4, col % 4
    me = core * 64 + x * COLS + col
    xs, zs, ys = ([v if d == 0 else wrap4(v + d) for d in range(4)] for v in (x, z, y))
    cols = {(dz, dy): zs[dz] * 4 + ys[dy] for dz in range(4) for dy in range(4)}
    xa, xb = jnp.where((z + y) % 2 == 0, xs[1], xs[3]), jnp.where((z + y) % 2 == 0, xs[3], xs[1])
    za, zb = jnp.where((x + y) % 2 == 0, zs[1], zs[3]), jnp.where((x + y) % 2 == 0, zs[3], zs[1])
    barrier = pltpu.get_barrier_semaphore()

    for dx, dz, dy in FAR_FIRST:
        for k in range(2):
            row2 = 2 * xs[dx] + (k if dx or dz or dy else 1 - core)
            if (dx, dz, dy) != (0, 0, 0) or k == 0:
                there = {"row": row2, "col": cols[dz, dy]}
                pl.semaphore_signal(barrier, inc=1, device_id=there, device_id_type=MESH)

    sends = ((s_lr0, s_t0), (s_lr1, s_t1))
    recvs = ((r_lr0, r_t0), (r_lr1, r_t1))

    def prepare_weights(t):
        for kind in range(4):
            w = wp_ref[t, :, kind * C : (kind + 1) * C].astype(F32).T.astype(BF16)
            for g in range(DEVICES // PLANE):
                wpt[g, kind * PLANE : (kind + 1) * PLANE, :] = w[g * PLANE : (g + 1) * PLANE]
        wgt[...] = wg_ref[t].astype(F32).T.astype(BF16)
        wot[t] = wo_ref[t].astype(F32).T.astype(BF16)
        wsum[t] = jnp.broadcast_to(jnp.sum(wot[t].astype(F32), axis=1, keepdims=True), (C, 128))

    def send(t, what, k, x2, c2, own, arrival):
        src, land = sends[t][what], recvs[t][what]
        slot = k * 64 + x2 * COLS + c2
        copy = pltpu.make_async_remote_copy(
            src_ref=src.at[slot],
            dst_ref=land.at[me],
            send_sem=send_sem.at[t, what, k],
            recv_sem=recv_sem.at[t, what, arrival],
            device_id={"row": 2 * x2 + k, "col": c2},
            device_id_type=MESH,
        )
        if own:
            keep = pltpu.make_async_copy(src.at[slot], land.at[me], send_sem.at[t, what, k])
            pl.when(core != k)(copy.start)
            pl.when(core == k)(keep.start)
        else:
            copy.start()

    def wait_sent(t, what, k):
        src = sends[t][what].at[pl.ds(0, 64)]
        pltpu.make_async_copy(src, src, send_sem.at[t, what, k]).wait()

    def wait_tiles(t, what, count, arrival):
        land = recvs[t][what].at[pl.ds(0, count)]
        pltpu.make_async_copy(land, land, recv_sem.at[t, what, arrival]).wait()

    def wait_triangle(t, k):
        @pl.when(core == k)
        def _():
            wait_sent(t, 1, k)
            wait_tiles(t, 1, 63, k)

        @pl.when(core != k)
        def _():
            wait_tiles(t, 1, 64, k)

    halves = ((xs[2], xa), (xb, xs[0]))

    def project(t, k, half):
        src = sends[t][0]
        size = PLANE * JH
        planes = halves[half]
        w = jnp.concatenate([wpt[k * 4 + x2] for x2 in planes], axis=0)
        for q in range(TOK // 256):
            v = jnp.dot(w, nt[:, q * 256 : (q + 1) * 256], preferred_element_type=F32)
            for p in range(2):
                for side in range(2):
                    at = p * 4 * PLANE + 2 * side * PLANE
                    proj = mask * sigmoid(v[at + PLANE : at + 2 * PLANE]) * v[at : at + PLANE]
                    for half in range(2):
                        to = (2 * p + side) * size + 2 * q + half
                        fbuf[pl.ds(to, PLANE, stride=JH), :] = proj[:, half * 128 : (half + 1) * 128]
        for p in range(2):
            for side in range(2):
                at = (2 * p + side) * size
                tiles = fbuf[at : at + size, :].astype(BF16).reshape(PLANE, JH, 128)
                src[pl.ds(k * 64 + planes[p] * COLS, PLANE), side] = tiles

    def send_half(t, k, half):
        for p, dz, dy in HALVES[half]:
            send(t, 0, k, halves[half][p], cols[dz, dy], (half, p, dz, dy) == (1, 1, 0, 0))

    def gates_of(t):
        for q in range(TOK // 256):
            sl = slice(q * 256, (q + 1) * 256)
            gate[:, sl] = mask * sigmoid(jnp.dot(wgt[...], nt[:, sl], preferred_element_type=F32))

    def triangle_and_send(t):
        land = recvs[t][0]
        src = sends[t][1]

        def relayout(offsets):
            for dx, dz, dy in offsets:
                x2, c = xs[dx], cols[dz, dy]
                slot = x2 * COLS + c
                rows = pl.ds(pl.multiple_of(c * CJ, CJ), JH), pl.ds(pl.multiple_of(c * CJ + JH, JH), JH)
                for side in range(2):
                    a, b = land[slot, side], land[64 + slot, side]
                    mat[side, x2, rows[0]] = jnp.concatenate([a[:, :64], b[:, :64]], axis=1)
                    mat[side, x2, rows[1]] = jnp.concatenate([a[:, 64:], b[:, 64:]], axis=1)

        far = [offset for offset in FAR_FIRST if hops(offset) >= 3]
        near = [offset for offset in FAR_FIRST if hops(offset) < 3]
        wait_tiles(t, 0, 2 * len(far), 0)
        relayout(far)
        wait_sent(t, 0, core)
        wait_tiles(t, 0, 2 * len(near) - 1, 1)
        relayout(near)
        left = jnp.concatenate([mat[0, x2] for x2 in range(4)], axis=1)
        for dz, z2 in ((2, zs[2]), (1, za), (3, zb), (0, zs[0])):
            if t == 0:
                v = lax.dot_general(mat[1, z2], left, (((0,), (0,)), ((), ())), preferred_element_type=F32)
            else:
                js = pl.ds(pl.multiple_of(z2 * 128, 128), 128)
                right = jnp.concatenate([mat[1, x2, js] for x2 in range(4)], axis=1)
                v = lax.dot_general(right, left, (((1,), (1,)), ((), ())), preferred_element_type=F32)
            v = v.astype(BF16)
            for k in range(2):
                for x2 in range(4):
                    lanes = slice(x2 * 128 + k * 64, x2 * 128 + (k + 1) * 64)
                    for y2 in range(4):
                        a = v[y2 * CJ : y2 * CJ + JH, lanes]
                        b = v[y2 * CJ + JH : (y2 + 1) * CJ, lanes]
                        src[k * 64 + x2 * COLS + z2 * 4 + y2] = jnp.concatenate([a, b], axis=1)
            for dx, dy in IN_PLANE:
                for k in range(2):
                    send(t, 1, k, xs[dx], z2 * 4 + ys[dy], (dx, dz, dy) == (0, 0, 0), core)

    def finish(t):
        back = recvs[t][1]

        zero = jnp.zeros((JH, 128), F32)

        def total(i, acc):
            new = []
            for n, a in enumerate(acc):
                h = 4 * i + n
                v = back[h].astype(F32)
                gbuf[pl.ds(pl.multiple_of(h * JH, JH), JH), :] = v
                new.append(a + v)
            return tuple(new)

        def square(i, acc):
            new = []
            for n, a in enumerate(acc):
                d = back[4 * i + n].astype(F32) - shift
                new.append(a + d * d)
            return tuple(new)

        def both(i, acc):
            new = []
            for n in range(4):
                h = 64 + 4 * i + n
                v = back[h].astype(F32)
                gbuf[pl.ds(pl.multiple_of(h * JH, JH), JH), :] = v
                d = v - shift
                new += [acc[2 * n] + d, acc[2 * n + 1] + d * d]
            return tuple(new)

        def product(j, k):
            tn = gbuf[pl.ds(k * 64 * JH + j, 64, stride=JH), :].astype(BF16)
            return jnp.dot(wot[t, :, k * 64 : (k + 1) * 64], tn, preferred_element_type=F32)

        wait_triangle(t, 0)
        acc = lax.fori_loop(0, 16, total, (zero,) * 4, unroll=4)
        shift = ((acc[0] + acc[1]) + (acc[2] + acc[3])) * (1.0 / 64)
        acc = lax.fori_loop(0, 16, square, (zero,) * 4, unroll=4)
        below = (acc[0] + acc[1]) + (acc[2] + acc[3])
        for j in range(JH):
            upd[:, j * 128 : (j + 1) * 128] = product(j, 0)
        wait_triangle(t, 1)
        acc = lax.fori_loop(0, 16, both, (zero,) * 8, unroll=4)
        delta = ((acc[0] + acc[2]) + (acc[4] + acc[6])) * (1.0 / DEVICES)
        square_sum = below + ((acc[1] + acc[3]) + (acc[5] + acc[7]))
        rstd = lax.rsqrt(square_sum * (1.0 / DEVICES) - delta * delta + EPS)
        mean = shift + delta
        for j in range(JH):
            sl = slice(j * 128, (j + 1) * 128)
            update = upd[:, sl] + product(j, 1) - wsum[t] * mean[j : j + 1]
            new = (pt[:, sl] + gate[:, sl] * (rstd[j : j + 1] * update)).astype(BF16).astype(F32)
            if t == 0:
                pt[:, sl] = new
                nt[:, sl] = norm_rows(new).astype(BF16)
            else:
                back_t = new.T
                xf[pl.ds(j, RI, stride=CJ), :] = back_t[:RI]
                xf[pl.ds(j + JH, RI, stride=CJ), :] = back_t[RI:]

    loads[0].wait()
    xf[...] = pair_ref[...].reshape(TOK, C).astype(F32)
    for j in range(JH):
        sl = slice(j * 128, (j + 1) * 128)
        tokens = jnp.concatenate(
            [xf[pl.ds(j, RI, stride=CJ), :], xf[pl.ds(j + JH, RI, stride=CJ), :]], axis=0
        )
        v = tokens.T
        pt[:, sl] = v
        nt[:, sl] = norm_rows(v).astype(BF16)
    for load in loads[1:]:
        load.wait()
    mask = mask_ref[x, z].astype(F32)
    prepare_weights(0)
    project(0, 0, 0)
    pl.semaphore_wait(barrier, DEVICES - 1)
    for t in range(2):
        for k in range(2):
            for half in range(2):
                if (t, k, half) != (0, 0, 0):
                    project(t, k, half)
            for dx, dz, dy in FAR_FIRST:
                send(t, 0, k, xs[dx], cols[dz, dy], (dx, dz, dy) == (0, 0, 0), int(hops((dx, dz, dy)) < 3))
        gates_of(t)
        if t == 0:
            prepare_weights(1)
        triangle_and_send(t)
        finish(t)
        for what in range(2):
            wait_sent(t, what, 1 - core)
    out_ref[...] = xf[...].astype(BF16).reshape(RI, CJ, C)


def on_device(pair_in, proj_weight, gate_weight, out_weight, block_mask):
    lr = pltpu.VMEM((DEVICES, 2, JH, 128), BF16)
    tr = pltpu.VMEM((DEVICES, JH, 128), BF16)
    vmem = pl.BlockSpec(memory_space=pltpu.VMEM)
    hbm = pl.BlockSpec(memory_space=pltpu.HBM)
    return pl.pallas_call(
        kernel,
        out_shape=jax.ShapeDtypeStruct((RI, CJ, C), BF16),
        in_specs=[hbm] * 5,
        out_specs=vmem,
        scratch_shapes=[
            pltpu.VMEM(pair_in.shape, BF16),
            pltpu.VMEM(proj_weight.shape, BF16),
            pltpu.VMEM(gate_weight.shape, BF16),
            pltpu.VMEM(out_weight.shape, BF16),
            pltpu.SMEM(block_mask.shape, jnp.int32),
            pltpu.VMEM((TOK, C), F32),
            pltpu.VMEM((C, TOK), F32),
            pltpu.VMEM((C, TOK), BF16),
            pltpu.VMEM((C, TOK), F32),
            pltpu.VMEM((DEVICES // PLANE, 4 * PLANE, C), BF16),
            pltpu.VMEM((C, C), BF16),
            pltpu.VMEM((2, C, C), BF16),
            pltpu.VMEM((2, C, 128), F32),
            pltpu.VMEM((C, TOK), F32),
            pltpu.VMEM((4 * PLANE * JH, 128), F32),
            pltpu.VMEM((DEVICES * JH, 128), F32),
            pltpu.VMEM((2, 4, N, 128), BF16),
            lr, lr, lr, lr, tr, tr, tr, tr,
            pltpu.SemaphoreType.DMA((2, 2, 2)),
            pltpu.SemaphoreType.DMA((2, 2, 2)),
            pltpu.SemaphoreType.DMA((5,)),
        ],
        compiler_params=pltpu.CompilerParams(
            collective_id=0, has_side_effects=True, vmem_limit_bytes=40 * 2**20
        ),
        name="triangle_pair",
    )(*(pltpu.with_memory_space_constraint(v, pltpu.HBM) for v in (pair_in, proj_weight, gate_weight, out_weight, block_mask)))


def solution(mesh):
    placed = (P("row", "col", None), P(), P(), P(), P())
    return jax.shard_map(
        on_device, mesh=mesh, in_specs=placed, out_specs=P("row", "col", None), check_vma=False
    )
```

```python
import jax
import jax.numpy as jnp
from jax import lax
from jax.experimental import pallas as pl
from jax.experimental.pallas import tpu as pltpu
from jax.sharding import PartitionSpec as P

MESH = pl.DeviceIdType.MESH
F32 = jnp.float32
BF16 = jnp.bfloat16
EPS = 1e-5

ROWS, COLS = 8, 16
DEVICES = ROWS * COLS
N = 512
C = 128
RI, CJ = 64, 32
JH = 16
TOK = RI * CJ
JP = 24
XP = 40
PLANE = COLS


def hops(offset):
    return sum(min(d, 4 - d) for d in offset)


HALVES = [
    sorted(
        ((p, (a + b) % 4, a) for b in range(4) for a in range(4) for p in range(2)),
        key=lambda o: -(hop[o[0]] + hops(o[1:])),
    )
    for hop in ((2, 1), (1, 0))
]
IN_PLANE = sorted((((a + b) % 4, a) for b in range(4) for a in range(4)), key=lambda o: -hops(o))
FAR_FIRST = sorted(
    ((a, (a + b) % 4, (a + c) % 4) for b in range(4) for c in range(4) for a in range(4)),
    key=lambda offset: -hops(offset),
)


def sigmoid(v):
    return 0.5 * jnp.tanh(0.5 * v) + 0.5


def norm_rows(v):
    center = v - jnp.mean(v, axis=0, keepdims=True)
    var = jnp.mean(center * center, axis=0, keepdims=True)
    return center * lax.rsqrt(var + EPS)


def wrap4(v):
    return jnp.where(v >= 4, v - 4, v)


def kernel(
    pair_hbm, wp_hbm, wg_hbm, wo_hbm, mask_hbm, out_ref,
    pair_ref, wp_ref, wg_ref, wo_ref, mask_ref,
    xf, pt, nt, gate, wpt, wgt, wot, wsum, upd, fbuf, gbuf, mat,
    s_lr0, s_lr1, r_lr0, r_lr1, s_t0, s_t1, r_t0, r_t1,
    send_sem, recv_sem, load_sem,
):
    row, col = lax.axis_index("row"), lax.axis_index("col")
    loads = [
        pltpu.make_async_copy(src, dst, load_sem.at[i])
        for i, (src, dst) in enumerate(
            [(pair_hbm, pair_ref), (mask_hbm, mask_ref), (wp_hbm, wp_ref), (wg_hbm, wg_ref), (wo_hbm, wo_ref)]
        )
    ]
    for load in loads:
        load.start()
    x, core = row // 2, row % 2
    z, y = col // 4, col % 4
    me = core * 64 + x * COLS + col
    xs, zs, ys = ([v if d == 0 else wrap4(v + d) for d in range(4)] for v in (x, z, y))
    cols = {(dz, dy): zs[dz] * 4 + ys[dy] for dz in range(4) for dy in range(4)}
    xa, xb = jnp.where((z + y) % 2 == 0, xs[1], xs[3]), jnp.where((z + y) % 2 == 0, xs[3], xs[1])
    za, zb = jnp.where((x + y) % 2 == 0, zs[1], zs[3]), jnp.where((x + y) % 2 == 0, zs[3], zs[1])
    barrier = pltpu.get_barrier_semaphore()

    for dx, dz, dy in FAR_FIRST:
        for k in range(2):
            row2 = 2 * xs[dx] + (k if dx or dz or dy else 1 - core)
            if (dx, dz, dy) != (0, 0, 0) or k == 0:
                there = {"row": row2, "col": cols[dz, dy]}
                pl.semaphore_signal(barrier, inc=1, device_id=there, device_id_type=MESH)

    sends = ((s_lr0, s_t0), (s_lr1, s_t1))
    recvs = ((r_lr0, r_t0), (r_lr1, r_t1))

    def prepare_weights(t):
        for kind in range(4):
            w = wp_ref[t, :, kind * C : (kind + 1) * C].astype(F32).T.astype(BF16)
            for g in range(DEVICES // PLANE):
                wpt[g, kind * PLANE : (kind + 1) * PLANE, :] = w[g * PLANE : (g + 1) * PLANE]
        wgt[...] = wg_ref[t].astype(F32).T.astype(BF16)
        wot[t] = wo_ref[t].astype(F32).T.astype(BF16)
        wsum[t] = jnp.broadcast_to(jnp.sum(wot[t].astype(F32), axis=1, keepdims=True), (C, 128))

    def send(t, what, k, x2, c2, own, arrival):
        src, land = sends[t][what], recvs[t][what]
        slot = k * 64 + x2 * COLS + c2
        copy = pltpu.make_async_remote_copy(
            src_ref=src.at[slot],
            dst_ref=land.at[me],
            send_sem=send_sem.at[t, what, k],
            recv_sem=recv_sem.at[t, what, arrival],
            device_id={"row": 2 * x2 + k, "col": c2},
            device_id_type=MESH,
        )
        if own:
            keep = pltpu.make_async_copy(src.at[slot], land.at[me], send_sem.at[t, what, k])
            pl.when(core != k)(copy.start)
            pl.when(core == k)(keep.start)
        else:
            copy.start()

    def wait_sent(t, what, k):
        src = sends[t][what].at[pl.ds(0, 64)]
        pltpu.make_async_copy(src, src, send_sem.at[t, what, k]).wait()

    def wait_tiles(t, what, count, arrival):
        land = recvs[t][what].at[pl.ds(0, count)]
        pltpu.make_async_copy(land, land, recv_sem.at[t, what, arrival]).wait()

    def wait_triangle(t, k):
        @pl.when(core == k)
        def _():
            wait_sent(t, 1, k)
            wait_tiles(t, 1, 63, k)

        @pl.when(core != k)
        def _():
            wait_tiles(t, 1, 64, k)

    halves = ((xs[2], xa), (xb, xs[0]))

    def project(t, k, half):
        src = sends[t][0]
        size = PLANE * JP
        planes = halves[half]
        w = jnp.concatenate([wpt[k * 4 + x2] for x2 in planes], axis=0)
        for q in range(TOK // 256):
            v = jnp.dot(w, nt[:, q * 256 : (q + 1) * 256], preferred_element_type=F32)
            for p in range(2):
                for side in range(2):
                    at = p * 4 * PLANE + 2 * side * PLANE
                    proj = mask * sigmoid(v[at + PLANE : at + 2 * PLANE]) * v[at : at + PLANE]
                    for half in range(2):
                        to = (2 * p + side) * size + 2 * q + half
                        fbuf[pl.ds(to, PLANE, stride=JP), :] = proj[:, half * 128 : (half + 1) * 128]
        for p in range(2):
            for side in range(2):
                at = (2 * p + side) * size
                for h in range(PLANE):
                    tile = fbuf[at + h * JP : at + h * JP + JH, :].astype(BF16)
                    src[k * 64 + planes[p] * COLS + h, side] = tile

    def send_half(t, k, half):
        for p, dz, dy in HALVES[half]:
            send(t, 0, k, halves[half][p], cols[dz, dy], (half, p, dz, dy) == (1, 1, 0, 0))

    def gates_of(t):
        for q in range(TOK // 256):
            sl = slice(q * 256, (q + 1) * 256)
            gate[:, sl] = mask * sigmoid(jnp.dot(wgt[...], nt[:, sl], preferred_element_type=F32))

    def triangle_and_send(t):
        land = recvs[t][0]
        src = sends[t][1]

        def relayout(offsets):
            for dx, dz, dy in offsets:
                x2, c = xs[dx], cols[dz, dy]
                slot = x2 * COLS + c
                rows = pl.ds(pl.multiple_of(c * CJ, CJ), JH), pl.ds(pl.multiple_of(c * CJ + JH, JH), JH)
                for side in range(2):
                    a, b = land[slot, side], land[64 + slot, side]
                    mat[side, x2, rows[0]] = jnp.concatenate([a[:, :64], b[:, :64]], axis=1)
                    mat[side, x2, rows[1]] = jnp.concatenate([a[:, 64:], b[:, 64:]], axis=1)

        far = [offset for offset in FAR_FIRST if hops(offset) >= 3]
        near = [offset for offset in FAR_FIRST if hops(offset) < 3]
        wait_tiles(t, 0, 2 * len(far), 0)
        relayout(far)
        wait_sent(t, 0, core)
        wait_tiles(t, 0, 2 * len(near) - 1, 1)
        relayout(near)
        left = jnp.concatenate([mat[0, x2] for x2 in range(4)], axis=1)
        for dz, z2 in ((2, zs[2]), (1, za), (3, zb), (0, zs[0])):
            if t == 0:
                v = lax.dot_general(mat[1, z2], left, (((0,), (0,)), ((), ())), preferred_element_type=F32)
            else:
                js = pl.ds(pl.multiple_of(z2 * 128, 128), 128)
                right = jnp.concatenate([mat[1, x2, js] for x2 in range(4)], axis=1)
                v = lax.dot_general(right, left, (((1,), (1,)), ((), ())), preferred_element_type=F32)
            v = v.astype(BF16)
            for k in range(2):
                for x2 in range(4):
                    lanes = slice(x2 * 128 + k * 64, x2 * 128 + (k + 1) * 64)
                    for y2 in range(4):
                        a = v[y2 * CJ : y2 * CJ + JH, lanes]
                        b = v[y2 * CJ + JH : (y2 + 1) * CJ, lanes]
                        src[k * 64 + x2 * COLS + z2 * 4 + y2] = jnp.concatenate([a, b], axis=1)
            for dx, dy in IN_PLANE:
                for k in range(2):
                    send(t, 1, k, xs[dx], z2 * 4 + ys[dy], (dx, dz, dy) == (0, 0, 0), core)

    def finish(t):
        back = recvs[t][1]

        zero = jnp.zeros((JH, 128), F32)

        def total(i, acc):
            new = []
            for n, a in enumerate(acc):
                h = 4 * i + n
                v = back[h].astype(F32)
                gbuf[pl.ds(pl.multiple_of(h * JP, 8), JH), :] = v
                new.append(a + v)
            return tuple(new)

        def square(i, acc):
            new = []
            for n, a in enumerate(acc):
                d = back[4 * i + n].astype(F32) - shift
                new.append(a + d * d)
            return tuple(new)

        def both(i, acc):
            new = []
            for n in range(4):
                h = 64 + 4 * i + n
                v = back[h].astype(F32)
                gbuf[pl.ds(pl.multiple_of(h * JP, 8), JH), :] = v
                d = v - shift
                new += [acc[2 * n] + d, acc[2 * n + 1] + d * d]
            return tuple(new)

        def product(j, k):
            tn = gbuf[pl.ds(k * 64 * JP + j, 64, stride=JP), :].astype(BF16)
            return jnp.dot(wot[t, :, k * 64 : (k + 1) * 64], tn, preferred_element_type=F32)

        wait_triangle(t, 0)
        acc = lax.fori_loop(0, 16, total, (zero,) * 4, unroll=4)
        shift = ((acc[0] + acc[1]) + (acc[2] + acc[3])) * (1.0 / 64)
        acc = lax.fori_loop(0, 16, square, (zero,) * 4, unroll=4)
        below = (acc[0] + acc[1]) + (acc[2] + acc[3])
        for j in range(JH):
            upd[:, j * 128 : (j + 1) * 128] = product(j, 0)
        wait_triangle(t, 1)
        acc = lax.fori_loop(0, 16, both, (zero,) * 8, unroll=4)
        delta = ((acc[0] + acc[2]) + (acc[4] + acc[6])) * (1.0 / DEVICES)
        square_sum = below + ((acc[1] + acc[3]) + (acc[5] + acc[7]))
        rstd = lax.rsqrt(square_sum * (1.0 / DEVICES) - delta * delta + EPS)
        mean = shift + delta
        for j in range(JH):
            sl = slice(j * 128, (j + 1) * 128)
            update = upd[:, sl] + product(j, 1) - wsum[t] * mean[j : j + 1]
            new = (pt[:, sl] + gate[:, sl] * (rstd[j : j + 1] * update)).astype(BF16).astype(F32)
            if t == 0:
                pt[:, sl] = new
                nt[:, sl] = norm_rows(new).astype(BF16)
            else:
                back_t = new.T
                xf[pl.ds(j, RI, stride=XP), :] = back_t[:RI]
                xf[pl.ds(j + JH, RI, stride=XP), :] = back_t[RI:]

    loads[0].wait()
    for i in range(RI):
        xf[i * XP : i * XP + CJ, :] = pair_ref[i].astype(F32)
    for j in range(JH):
        sl = slice(j * 128, (j + 1) * 128)
        tokens = jnp.concatenate(
            [xf[pl.ds(j, RI, stride=XP), :], xf[pl.ds(j + JH, RI, stride=XP), :]], axis=0
        )
        v = tokens.T
        pt[:, sl] = v
        nt[:, sl] = norm_rows(v).astype(BF16)
    for load in loads[1:]:
        load.wait()
    mask = mask_ref[x, z].astype(F32)
    prepare_weights(0)
    project(0, 0, 0)
    pl.semaphore_wait(barrier, DEVICES - 1)
    for t in range(2):
        for k in range(2):
            for half in range(2):
                if (t, k, half) != (0, 0, 0):
                    project(t, k, half)
            for dx, dz, dy in FAR_FIRST:
                send(t, 0, k, xs[dx], cols[dz, dy], (dx, dz, dy) == (0, 0, 0), int(hops((dx, dz, dy)) < 3))
        gates_of(t)
        if t == 0:
            prepare_weights(1)
        triangle_and_send(t)
        finish(t)
        for what in range(2):
            wait_sent(t, what, 1 - core)
    for i in range(RI):
        out_ref[i] = xf[i * XP : i * XP + CJ, :].astype(BF16)


def on_device(pair_in, proj_weight, gate_weight, out_weight, block_mask):
    lr = pltpu.VMEM((DEVICES, 2, JH, 128), BF16)
    tr = pltpu.VMEM((DEVICES, JH, 128), BF16)
    vmem = pl.BlockSpec(memory_space=pltpu.VMEM)
    hbm = pl.BlockSpec(memory_space=pltpu.HBM)
    return pl.pallas_call(
        kernel,
        out_shape=jax.ShapeDtypeStruct((RI, CJ, C), BF16),
        in_specs=[hbm] * 5,
        out_specs=vmem,
        scratch_shapes=[
            pltpu.VMEM(pair_in.shape, BF16),
            pltpu.VMEM(proj_weight.shape, BF16),
            pltpu.VMEM(gate_weight.shape, BF16),
            pltpu.VMEM(out_weight.shape, BF16),
            pltpu.SMEM(block_mask.shape, jnp.int32),
            pltpu.VMEM((RI * XP, C), F32),
            pltpu.VMEM((C, TOK), F32),
            pltpu.VMEM((C, TOK), BF16),
            pltpu.VMEM((C, TOK), F32),
            pltpu.VMEM((DEVICES // PLANE, 4 * PLANE, C), BF16),
            pltpu.VMEM((C, C), BF16),
            pltpu.VMEM((2, C, C), BF16),
            pltpu.VMEM((2, C, 128), F32),
            pltpu.VMEM((C, TOK), F32),
            pltpu.VMEM((4 * PLANE * JP, 128), F32),
            pltpu.VMEM((DEVICES * JP, 128), F32),
            pltpu.VMEM((2, 4, N, 128), BF16),
            lr, lr, lr, lr, tr, tr, tr, tr,
            pltpu.SemaphoreType.DMA((2, 2, 2)),
            pltpu.SemaphoreType.DMA((2, 2, 2)),
            pltpu.SemaphoreType.DMA((5,)),
        ],
        compiler_params=pltpu.CompilerParams(
            collective_id=0, has_side_effects=True, vmem_limit_bytes=40 * 2**20
        ),
        name="triangle_pair",
    )(*(pltpu.with_memory_space_constraint(v, pltpu.HBM) for v in (pair_in, proj_weight, gate_weight, out_weight, block_mask)))


def solution(mesh):
    placed = (P("row", "col", None), P(), P(), P(), P())
    return jax.shard_map(
        on_device, mesh=mesh, in_specs=placed, out_specs=P("row", "col", None), check_vma=False
    )
```

```python
import jax
import jax.numpy as jnp
from jax import lax
from jax.experimental import pallas as pl
from jax.experimental.pallas import tpu as pltpu
from jax.sharding import PartitionSpec as P

MESH = pl.DeviceIdType.MESH
F32 = jnp.float32
BF16 = jnp.bfloat16
EPS = 1e-5

ROWS, COLS = 8, 16
DEVICES = ROWS * COLS
N = 512
C = 128
RI, CJ = 64, 32
JH = 16
TOK = RI * CJ
JP = 24
XP = 40
PLANE = COLS


def hops(offset):
    return sum(min(d, 4 - d) for d in offset)


HALVES = [
    sorted(
        ((p, (a + b) % 4, a) for b in range(4) for a in range(4) for p in range(2)),
        key=lambda o: -(hop[o[0]] + hops(o[1:])),
    )
    for hop in ((2, 1), (1, 0))
]
IN_PLANE = sorted((((a + b) % 4, a) for b in range(4) for a in range(4)), key=lambda o: -hops(o))
FAR_FIRST = sorted(
    ((a, (a + b) % 4, (a + c) % 4) for b in range(4) for c in range(4) for a in range(4)),
    key=lambda offset: -hops(offset),
)


def sigmoid(v):
    return 0.5 * jnp.tanh(0.5 * v) + 0.5


def norm_rows(v):
    center = v - jnp.mean(v, axis=0, keepdims=True)
    var = jnp.mean(center * center, axis=0, keepdims=True)
    return center * lax.rsqrt(var + EPS)


def wrap4(v):
    return jnp.where(v >= 4, v - 4, v)


def kernel(
    pair_hbm, wp_hbm, wg_hbm, wo_hbm, mask_hbm, out_ref,
    pair_ref, wp_ref, wg_ref, wo_ref, mask_ref,
    xf, pt, nt, gate, wpt, wgt, wot, wsum, upd, fbuf, gbuf, mat,
    s_lr0, s_lr1, r_lr0, r_lr1, s_t0, s_t1, r_t0, r_t1,
    send_sem, recv_sem, load_sem,
):
    row, col = lax.axis_index("row"), lax.axis_index("col")
    loads = [
        pltpu.make_async_copy(src, dst, load_sem.at[i])
        for i, (src, dst) in enumerate(
            [(pair_hbm, pair_ref), (mask_hbm, mask_ref), (wp_hbm, wp_ref), (wg_hbm, wg_ref), (wo_hbm, wo_ref)]
        )
    ]
    for load in loads:
        load.start()
    x, core = row // 2, row % 2
    z, y = col // 4, col % 4
    me = core * 64 + x * COLS + col
    xs, zs, ys = ([v if d == 0 else wrap4(v + d) for d in range(4)] for v in (x, z, y))
    cols = {(dz, dy): zs[dz] * 4 + ys[dy] for dz in range(4) for dy in range(4)}
    xa, xb = jnp.where((z + y) % 2 == 0, xs[1], xs[3]), jnp.where((z + y) % 2 == 0, xs[3], xs[1])
    za, zb = jnp.where((x + y) % 2 == 0, zs[1], zs[3]), jnp.where((x + y) % 2 == 0, zs[3], zs[1])
    barrier = pltpu.get_barrier_semaphore()

    for dx, dz, dy in FAR_FIRST:
        for k in range(2):
            row2 = 2 * xs[dx] + (k if dx or dz or dy else 1 - core)
            if (dx, dz, dy) != (0, 0, 0) or k == 0:
                there = {"row": row2, "col": cols[dz, dy]}
                pl.semaphore_signal(barrier, inc=1, device_id=there, device_id_type=MESH)

    sends = ((s_lr0, s_t0), (s_lr1, s_t1))
    recvs = ((r_lr0, r_t0), (r_lr1, r_t1))

    def prepare_weights(t):
        for kind in range(4):
            w = wp_ref[t, :, kind * C : (kind + 1) * C].astype(F32).T.astype(BF16)
            for g in range(DEVICES // PLANE):
                wpt[g, kind * PLANE : (kind + 1) * PLANE, :] = w[g * PLANE : (g + 1) * PLANE]
        wgt[...] = wg_ref[t].astype(F32).T.astype(BF16)
        wot[t] = wo_ref[t].astype(F32).T.astype(BF16)
        wsum[t] = jnp.broadcast_to(jnp.sum(wot[t].astype(F32), axis=1, keepdims=True), (C, 128))

    def send(t, what, k, x2, c2, own, arrival):
        src, land = sends[t][what], recvs[t][what]
        slot = k * 64 + x2 * COLS + c2
        copy = pltpu.make_async_remote_copy(
            src_ref=src.at[slot],
            dst_ref=land.at[me],
            send_sem=send_sem.at[t, what, k],
            recv_sem=recv_sem.at[t, what, arrival],
            device_id={"row": 2 * x2 + k, "col": c2},
            device_id_type=MESH,
        )
        if own:
            keep = pltpu.make_async_copy(src.at[slot], land.at[me], send_sem.at[t, what, k])
            pl.when(core != k)(copy.start)
            pl.when(core == k)(keep.start)
        else:
            copy.start()

    def wait_sent(t, what, k):
        src = sends[t][what].at[pl.ds(0, 64)]
        pltpu.make_async_copy(src, src, send_sem.at[t, what, k]).wait()

    def wait_tiles(t, what, count, arrival):
        land = recvs[t][what].at[pl.ds(0, count)]
        pltpu.make_async_copy(land, land, recv_sem.at[t, what, arrival]).wait()

    def wait_triangle(t, k):
        @pl.when(core == k)
        def _():
            wait_sent(t, 1, k)
            wait_tiles(t, 1, 63, k)

        @pl.when(core != k)
        def _():
            wait_tiles(t, 1, 64, k)

    halves = ((xs[2], xa), (xb, xs[0]))

    def project(t, k, half):
        src = sends[t][0]
        size = PLANE * JP
        planes = halves[half]
        w = jnp.concatenate([wpt[k * 4 + x2] for x2 in planes], axis=0)
        for q in range(TOK // 256):
            v = jnp.dot(w, nt[:, q * 256 : (q + 1) * 256], preferred_element_type=F32)
            for p in range(2):
                for side in range(2):
                    at = p * 4 * PLANE + 2 * side * PLANE
                    proj = mask * sigmoid(v[at + PLANE : at + 2 * PLANE]) * v[at : at + PLANE]
                    for half in range(2):
                        to = (2 * p + side) * size + 2 * q + half
                        fbuf[pl.ds(to, PLANE, stride=JP), :] = proj[:, half * 128 : (half + 1) * 128]
        for p in range(2):
            for side in range(2):
                at = (2 * p + side) * size
                for h in range(PLANE):
                    tile = fbuf[at + h * JP : at + h * JP + JH, :].astype(BF16)
                    src[k * 64 + planes[p] * COLS + h, side] = tile

    def send_half(t, k, half):
        for p, dz, dy in HALVES[half]:
            send(t, 0, k, halves[half][p], cols[dz, dy], (half, p, dz, dy) == (1, 1, 0, 0))

    def gates_of(t):
        for q in range(TOK // 256):
            sl = slice(q * 256, (q + 1) * 256)
            gate[:, sl] = mask * sigmoid(jnp.dot(wgt[...], nt[:, sl], preferred_element_type=F32))

    def triangle_and_send(t):
        land = recvs[t][0]
        src = sends[t][1]

        def relayout(offsets):
            for dx, dz, dy in offsets:
                x2, c = xs[dx], cols[dz, dy]
                slot = x2 * COLS + c
                rows = pl.ds(pl.multiple_of(c * CJ, CJ), JH), pl.ds(pl.multiple_of(c * CJ + JH, JH), JH)
                for side in range(2):
                    a, b = land[slot, side], land[64 + slot, side]
                    mat[side, x2, rows[0]] = jnp.concatenate([a[:, :64], b[:, :64]], axis=1)
                    mat[side, x2, rows[1]] = jnp.concatenate([a[:, 64:], b[:, 64:]], axis=1)

        far = [offset for offset in FAR_FIRST if hops(offset) >= 3]
        near = [offset for offset in FAR_FIRST if hops(offset) < 3]
        wait_tiles(t, 0, 2 * len(far), 0)
        relayout(far)
        wait_sent(t, 0, core)
        wait_tiles(t, 0, 2 * len(near) - 1, 1)
        relayout(near)
        left = jnp.concatenate([mat[0, x2] for x2 in range(4)], axis=1)
        for dz, z2 in ((2, zs[2]), (1, za), (3, zb), (0, zs[0])):
            if t == 0:
                v = lax.dot_general(mat[1, z2], left, (((0,), (0,)), ((), ())), preferred_element_type=F32)
            else:
                js = pl.ds(pl.multiple_of(z2 * 128, 128), 128)
                right = jnp.concatenate([mat[1, x2, js] for x2 in range(4)], axis=1)
                v = lax.dot_general(right, left, (((1,), (1,)), ((), ())), preferred_element_type=F32)
            v = v.astype(BF16)
            for k in range(2):
                for x2 in range(4):
                    lanes = slice(x2 * 128 + k * 64, x2 * 128 + (k + 1) * 64)
                    for y2 in range(4):
                        a = v[y2 * CJ : y2 * CJ + JH, lanes]
                        b = v[y2 * CJ + JH : (y2 + 1) * CJ, lanes]
                        src[k * 64 + x2 * COLS + z2 * 4 + y2] = jnp.concatenate([a, b], axis=1)
            for dx, dy in IN_PLANE:
                for k in range(2):
                    send(t, 1, k, xs[dx], z2 * 4 + ys[dy], (dx, dz, dy) == (0, 0, 0), core)

    def finish(t):
        back = recvs[t][1]

        zero = jnp.zeros((JH, 128), F32)

        def total(i, acc):
            new = []
            for n, a in enumerate(acc):
                h = 4 * i + n
                v = back[h].astype(F32)
                gbuf[pl.ds(pl.multiple_of(h * JP, 8), JH), :] = v
                new.append(a + v)
            return tuple(new)

        def square(i, acc):
            new = []
            for n, a in enumerate(acc):
                d = back[4 * i + n].astype(F32) - shift
                new.append(a + d * d)
            return tuple(new)

        def both(i, acc):
            new = []
            for n in range(4):
                h = 64 + 4 * i + n
                v = back[h].astype(F32)
                gbuf[pl.ds(pl.multiple_of(h * JP, 8), JH), :] = v
                d = v - shift
                new += [acc[2 * n] + d, acc[2 * n + 1] + d * d]
            return tuple(new)

        def product(j, k):
            tn = jnp.concatenate(
                [gbuf[pl.ds(k * 64 * JP + n, 64, stride=JP), :].astype(BF16) for n in (j, j + 1)], axis=1
            )
            return jnp.dot(wot[t, :, k * 64 : (k + 1) * 64], tn, preferred_element_type=F32)

        wait_triangle(t, 0)
        acc = lax.fori_loop(0, 16, total, (zero,) * 4, unroll=4)
        shift = ((acc[0] + acc[1]) + (acc[2] + acc[3])) * (1.0 / 64)
        acc = lax.fori_loop(0, 16, square, (zero,) * 4, unroll=4)
        below = (acc[0] + acc[1]) + (acc[2] + acc[3])
        for j in range(0, JH, 2):
            upd[:, j * 128 : (j + 2) * 128] = product(j, 0)
        wait_triangle(t, 1)
        acc = lax.fori_loop(0, 16, both, (zero,) * 8, unroll=4)
        delta = ((acc[0] + acc[2]) + (acc[4] + acc[6])) * (1.0 / DEVICES)
        square_sum = below + ((acc[1] + acc[3]) + (acc[5] + acc[7]))
        rstd = lax.rsqrt(square_sum * (1.0 / DEVICES) - delta * delta + EPS)
        mean = shift + delta
        for j in range(JH):
            sl = slice(j * 128, (j + 1) * 128)
            if j % 2 == 0:
                pair = product(j, 1)
            update = upd[:, sl] + pair[:, j % 2 * 128 : (j % 2 + 1) * 128] - wsum[t] * mean[j : j + 1]
            new = (pt[:, sl] + gate[:, sl] * (rstd[j : j + 1] * update)).astype(BF16).astype(F32)
            if t == 0:
                pt[:, sl] = new
                nt[:, sl] = norm_rows(new).astype(BF16)
            else:
                back_t = new.T
                xf[pl.ds(j, RI, stride=XP), :] = back_t[:RI]
                xf[pl.ds(j + JH, RI, stride=XP), :] = back_t[RI:]

    loads[0].wait()
    for i in range(RI):
        xf[i * XP : i * XP + CJ, :] = pair_ref[i].astype(F32)
    for j in range(JH):
        sl = slice(j * 128, (j + 1) * 128)
        tokens = jnp.concatenate(
            [xf[pl.ds(j, RI, stride=XP), :], xf[pl.ds(j + JH, RI, stride=XP), :]], axis=0
        )
        v = tokens.T
        pt[:, sl] = v
        nt[:, sl] = norm_rows(v).astype(BF16)
    for load in loads[1:]:
        load.wait()
    mask = mask_ref[x, z].astype(F32)
    prepare_weights(0)
    project(0, 0, 0)
    pl.semaphore_wait(barrier, DEVICES - 1)
    for t in range(2):
        for k in range(2):
            for half in range(2):
                if (t, k, half) != (0, 0, 0):
                    project(t, k, half)
            for dx, dz, dy in FAR_FIRST:
                send(t, 0, k, xs[dx], cols[dz, dy], (dx, dz, dy) == (0, 0, 0), int(hops((dx, dz, dy)) < 3))
        gates_of(t)
        if t == 0:
            prepare_weights(1)
        triangle_and_send(t)
        finish(t)
        for what in range(2):
            wait_sent(t, what, 1 - core)
    for i in range(RI):
        out_ref[i] = xf[i * XP : i * XP + CJ, :].astype(BF16)


def on_device(pair_in, proj_weight, gate_weight, out_weight, block_mask):
    lr = pltpu.VMEM((DEVICES, 2, JH, 128), BF16)
    tr = pltpu.VMEM((DEVICES, JH, 128), BF16)
    vmem = pl.BlockSpec(memory_space=pltpu.VMEM)
    hbm = pl.BlockSpec(memory_space=pltpu.HBM)
    return pl.pallas_call(
        kernel,
        out_shape=jax.ShapeDtypeStruct((RI, CJ, C), BF16),
        in_specs=[hbm] * 5,
        out_specs=vmem,
        scratch_shapes=[
            pltpu.VMEM(pair_in.shape, BF16),
            pltpu.VMEM(proj_weight.shape, BF16),
            pltpu.VMEM(gate_weight.shape, BF16),
            pltpu.VMEM(out_weight.shape, BF16),
            pltpu.SMEM(block_mask.shape, jnp.int32),
            pltpu.VMEM((RI * XP, C), F32),
            pltpu.VMEM((C, TOK), F32),
            pltpu.VMEM((C, TOK), BF16),
            pltpu.VMEM((C, TOK), F32),
            pltpu.VMEM((DEVICES // PLANE, 4 * PLANE, C), BF16),
            pltpu.VMEM((C, C), BF16),
            pltpu.VMEM((2, C, C), BF16),
            pltpu.VMEM((2, C, 128), F32),
            pltpu.VMEM((C, TOK), F32),
            pltpu.VMEM((4 * PLANE * JP, 128), F32),
            pltpu.VMEM((DEVICES * JP, 128), F32),
            pltpu.VMEM((2, 4, N, 128), BF16),
            lr, lr, lr, lr, tr, tr, tr, tr,
            pltpu.SemaphoreType.DMA((2, 2, 2)),
            pltpu.SemaphoreType.DMA((2, 2, 2)),
            pltpu.SemaphoreType.DMA((5,)),
        ],
        compiler_params=pltpu.CompilerParams(
            collective_id=0, has_side_effects=True, vmem_limit_bytes=40 * 2**20
        ),
        name="triangle_pair",
    )(*(pltpu.with_memory_space_constraint(v, pltpu.HBM) for v in (pair_in, proj_weight, gate_weight, out_weight, block_mask)))


def solution(mesh):
    placed = (P("row", "col", None), P(), P(), P(), P())
    return jax.shard_map(
        on_device, mesh=mesh, in_specs=placed, out_specs=P("row", "col", None), check_vma=False
    )
```
